512 devices in a mesh: shift: 4 (over x), cells: 128 (over z, y, core).
Axes of the slice: x: 4, y: 4, z: 16, core: 2. Of those that a mesh axis runs over, the one named last changes fastest.
Arguments:
- perm: float32 [1024, 64, 256], P(('shift', 'cells')), parts along dimension 0, may hold values from 0.1 to 10
- storage: float32 [1024, 64, 256], P(('shift', 'cells')), parts along dimension 0, may hold values from 0.005 to 0.05
- right_side: float32 [1024, 64, 256], P(('shift', 'cells')), parts along dimension 0, may hold values from -15 to 15
- coupling: bfloat16 [16384, 64, 256], P('cells'), may hold values from -0.75 to 0.75
- gains: bfloat16 [16384, 64], P('cells'), may hold values from 0.5 to 2
- well_target: int32 [16384, 1], P('cells'), may hold values from 0 to 127; in each aligned block of 128 rows (0 to 127, 128 to 255, ...) at most 2 rows name the same one
- well_column: int32 [16384], P('cells'), may hold values from 0 to 127
Outputs:
- solution: float32 [1024, 64, 256], P(('shift', 'cells')), parts along dimension 0
- residual: float32 [1024, 64, 256], P(('shift', 'cells')), parts along dimension 0
The draws below stay inside these ranges and needn't reach their ends.
There are 4 independent parts, one for each index of `shift`. The reference program is written for one: setup_inputs(seed, part) draws one part's arguments, and reference() takes and returns one part's arrays. A program takes and returns all parts, laid end to end along the dimension named above; an argument that names none is the same for every part. Nothing has to cross between parts.
Inputs may be any that keep to these rules, and one draw needn't show every extreme that they name: `well_target`: among the completions listed on one device, at most 2 name the same cell block, and some device has 2 naming one block.
All inputs are finite; a program needn't handle non-finite values.
Results may differ from the reference program's by a relative error of at most 0.0045.
Values may be sent and summed in bfloat16 or wider, within the bound.
A program may use at most 128 MiB of HBM per device.

```python
import math
import jax
import jax.numpy as jnp
import numpy as np
from jax import lax

CX = 2
NY = 64
NZ = 256
PERF = 64
COMP_DEV = 128
ITERS = 2
NX = 256
COLS = 128
CAP = 2
COMPL = 16384
N_CELLS = 128


def draw_right_side(key, part):
    ramp = 1.0 + 2.0 * jnp.arange(NX, dtype=jnp.float32)[:, None, None] / NX
    base = jnp.clip(jax.random.normal(key, (NX, NY, NZ), jnp.float32), -5.0, 5.0)
    result = ramp * base
    return result


def with_ends(entries, key, smallest, largest):
    longest = entries.shape.index(max(entries.shape))
    spots = []
    for shift in (0, 1):
        where = [jax.random.randint(jax.random.fold_in(key, axis), (), 0, length) for axis, length in enumerate(entries.shape)]
        where[longest] = (where[longest] + shift) % entries.shape[longest]
        spots.append(tuple(where))
    return entries.at[spots[0]].set(smallest).at[spots[1]].set(largest)


def levels(rng, dims, split, least, high):
    gain, own = 1.0, jax.random.fold_in(rng, 6)
    for dim, shards_of in split:
        heights = jnp.exp(jax.random.uniform(jax.random.fold_in(own, dim), (shards_of,), jnp.float32, least / len(split), high / len(split)))
        gain = gain * jnp.repeat(heights, dims[dim] // shards_of).reshape([-1 if axis == dim else 1 for axis in range(len(dims))])
    return gain


def shared_out(own_key, own, number, rows, amount, top, reach, lean):
    order = jax.random.permutation(own_key, amount)
    heavy_load, usual = load_shares(amount, rows * top, reach, lean, True), load_shares(amount, rows * top, reach, lean, False)
    places = jnp.arange(amount)

    def named(tallies, rotation):
        used = int((tallies > 0).sum())
        fixed = max(1, used // 4)
        moved = fixed + (places - fixed + rotation * (used - fixed)) % max(1, amount - fixed)
        return jnp.zeros((amount,), jnp.int32).at[order[jnp.where(places < fixed, places, moved)]].set(jnp.asarray(tallies, jnp.int32))

    tallies = jnp.where(number % 4 == 0, named(heavy_load, number // 4), named(usual, number - number // 4 - 1))
    mixed = jax.random.permutation(jax.random.fold_in(own, 3), amount)
    source_of, receiver = mixed[0:amount // 2 * 2:2], mixed[1:amount // 2 * 2:2]
    margin = jnp.minimum(tallies[source_of] - 1, reach - tallies[receiver]) // 2
    margin = jnp.where((source_of == order[0]) | (receiver == order[0]) | (tallies[receiver] == 0), 0, jnp.maximum(margin, 0))
    moved = jax.random.randint(jax.random.fold_in(own, 4), (amount // 2,), 0, 1 << 20) % (margin + 1)
    tallies = tallies.at[source_of].add(-moved).at[receiver].add(moved)
    items = jnp.searchsorted(jnp.cumsum(tallies), jnp.arange(rows * top), side="right").astype(jnp.int32)
    listing = items.reshape(top, rows).T
    listing = listing[jax.random.permutation(jax.random.fold_in(own, 1), rows)]
    rotation = jax.random.randint(jax.random.fold_in(own, 2), (rows, 1), 0, top)
    return jnp.take_along_axis(listing, (jnp.arange(top)[None, :] + rotation) % top, axis=1)


def load_shares(amount, total, reach, slope, full):
    portions = [(1 << 20) // math.isqrt(grade ** slope) + 1 for grade in range(1, amount + 1)]
    largest = reach if full else min(reach, max(-(-total // amount), total * portions[0] // sum(portions)))
    least = 1 if total - largest >= amount - 1 else 0
    counts, spare = [largest] + [least] * (amount - 1), total - largest - least * (amount - 1)
    while spare > 0:
        free = [i for i in range(1, amount) if counts[i] < largest] or [i for i in range(1, amount) if counts[i] < reach]
        whole, remaining = sum([portions[i] for i in free]), spare
        for i in free:
            addition = min(reach - counts[i], max(1, remaining * portions[i] // whole), spare)
            counts[i] = counts[i] + addition
            spare = spare - addition
    return np.array(counts)


def bell_draw(rng, dims, spread, most, cuts=(), kind=jnp.bfloat16):
    values = jax.random.normal(rng, dims, jnp.float32) * spread
    if len(cuts) > 0:
        values = levels(rng, dims, cuts, -0.22, 0.18) * values
    return jnp.clip(values, min=-most, max=most).astype(kind)


def setup_inputs(seed: int = 0, part: int = 0) -> dict:
    keys = jax.random.split(jax.random.key(seed), 8)
    part_keys = jax.random.split(jax.random.fold_in(keys[7], part), 8)
    perm = jnp.clip(jnp.exp(math.log(10.0) - 4.6051702 * jax.random.uniform(part_keys[0], (NX, NY, NZ), jnp.float32) ** levels(part_keys[0], (NX, NY, NZ), ((0, 128),), -0.2, 0.2)), 0.1, 10.0)
    storage = jnp.clip(jnp.exp(math.log(0.05) - 2.3025851 * jax.random.uniform(part_keys[1], (NX, NY, NZ), jnp.float32) ** levels(part_keys[1], (NX, NY, NZ), ((0, 128),), -0.2, 0.2)), 0.005, 0.05)
    right_side = draw_right_side(jax.random.fold_in(jax.random.fold_in(keys[7], part), 71), part)
    coupling = bell_draw(keys[3], (COMPL, PERF, NZ), PERF ** -0.5, 0.75, ((0, 128),))
    gains = jnp.clip(jnp.exp(math.log(2.0) - 1.3862944 * jax.random.uniform(keys[4], (COMPL, PERF), jnp.float32) ** levels(keys[4], (COMPL, PERF), ((0, 128),), -0.2, 0.2)), 0.5, 2.0).astype(jnp.bfloat16)
    well_target_keys = jax.random.split(jax.random.fold_in(keys[5], 1), COMPL // COMP_DEV)
    well_target_turns = jax.random.permutation(jax.random.fold_in(keys[5], 3), COMPL // COMP_DEV)
    well_target = jax.vmap(lambda own, number: shared_out(jax.random.fold_in(keys[5], 2), own, number, COMP_DEV, N_CELLS, 1, CAP, 2))(well_target_keys, well_target_turns).reshape((COMPL, 1))
    well_column = with_ends(jax.random.randint(keys[6], (COMPL,), 0, CX * NY), jax.random.fold_in(keys[6], 1), 0, (CX * NY) - 1).astype(jnp.int32)
    return dict(perm=perm, storage=storage, right_side=right_side, coupling=coupling, gains=gains, well_target=well_target, well_column=well_column)


def harmonic(first, second):
    return 2.0 * first * second / (first + second)

def face_values(perm):
    pad_x = jnp.pad(perm, ((1, 1), (0, 0), (0, 0)))
    pad_y = jnp.pad(perm, ((0, 0), (1, 1), (0, 0)))
    pad_z = jnp.pad(perm, ((0, 0), (0, 0), (1, 1)))
    trans_x = harmonic(pad_x[:-1], pad_x[1:])
    trans_y = harmonic(pad_y[:, :-1], pad_y[:, 1:])
    trans_z = harmonic(pad_z[:, :, :-1], pad_z[:, :, 1:])
    return (trans_x, trans_y, trans_z)

def precondition(values, trans_z, diagonal):
    lower = -trans_z[:, :, :-1]
    upper = -trans_z[:, :, 1:]
    return lax.linalg.tridiagonal_solve(lower, diagonal, upper, values[..., None])[..., 0]

def reference(perm, storage, right_side, coupling, gains, well_target, well_column):
    trans_x, trans_y, trans_z = face_values(perm)
    diagonal = storage + trans_x[:-1] + trans_x[1:] + trans_y[:, :-1] + trans_y[:, 1:] + trans_z[:, :, :-1] + trans_z[:, :, 1:]
    global_cols = (well_target[:, 0].astype(jnp.int32) * COLS + well_column.astype(jnp.int32)).astype(jnp.int32)
    block_coupling = coupling.reshape(N_CELLS, COMP_DEV, PERF, NZ)
    block_gains = gains.reshape(N_CELLS, COMP_DEV, PERF)
    block_cols = global_cols.reshape(N_CELLS, COMP_DEV)

    def well_term(field):
        field_cols = field.reshape(NX * NY, NZ)

        def add_group(total, pieces):
            blk, gain_rows, indices = pieces
            rows = lax.optimization_barrier(field_cols[indices].astype(jnp.bfloat16)).astype(jnp.float32)
            wide = blk.astype(jnp.float32)
            proj = jnp.einsum('kpc,kc->kp', wide, rows, precision=lax.Precision.HIGHEST)
            scaled = lax.optimization_barrier((proj * gain_rows.astype(jnp.float32)).astype(jnp.bfloat16)).astype(jnp.float32)
            back = jnp.einsum('kpc,kp->kc', wide, scaled, precision=lax.Precision.HIGHEST)
            return (total.at[indices].add(back), None)
        start = jnp.zeros((NX * NY, NZ), jnp.float32)
        total, _ = lax.scan(add_group, start, (block_coupling, block_gains, block_cols))
        return total.reshape(NX, NY, NZ)

    def operate(field):
        pad_x = jnp.pad(field, ((1, 1), (0, 0), (0, 0)))
        pad_y = jnp.pad(field, ((0, 0), (1, 1), (0, 0)))
        pad_z = jnp.pad(field, ((0, 0), (0, 0), (1, 1)))
        result = diagonal * field - trans_x[:-1] * pad_x[:-2] - trans_x[1:] * pad_x[2:]
        result = result - trans_y[:, :-1] * pad_y[:, :-2] - trans_y[:, 1:] * pad_y[:, 2:]
        result = result - trans_z[:, :, :-1] * pad_z[:, :, :-2] - trans_z[:, :, 1:] * pad_z[:, :, 2:]
        return result + well_term(field)
    solution = jnp.zeros_like(right_side)
    residual = right_side
    smoothed = precondition(residual, trans_z, diagonal)
    direction = smoothed
    norm_now = jnp.sum(residual * smoothed)
    for iteration in range(ITERS):
        image = operate(direction)
        alpha = norm_now / jnp.sum(direction * image)
        solution = solution + alpha * direction
        residual = residual - alpha * image
        if iteration + 1 < ITERS:
            smoothed = precondition(residual, trans_z, diagonal)
            fresh = jnp.sum(residual * smoothed)
            direction = smoothed + fresh / norm_now * direction
            norm_now = fresh
    return (solution, residual)
```

```python
import functools

import jax
import jax.numpy as jnp
from jax import lax
from jax.experimental import pallas as pl
from jax.experimental.pallas import tpu as pltpu
from jax.sharding import PartitionSpec as P

F32 = jnp.float32
BF16 = jnp.bfloat16
LANES = 128
GROUP = 16
ALONG_Y = 4
LARGEST = 32767.0


def nt(a, b):
    return lax.dot_general(a, b, (((1,), (1,)), ((), ())), preferred_element_type=F32)


def nn(a, b):
    return lax.dot_general(a, b, (((1,), (0,)), ((), ())), preferred_element_type=F32)


def iota(shape, dim):
    return lax.broadcasted_iota(jnp.int32, shape, dim)


def harmonic(first, second):
    return 2.0 * first * second / (first + second)


def up(v, k, axis=0):
    return pltpu.roll(v, k, axis)


def down(v, k, axis=0):
    return pltpu.roll(v, v.shape[axis] - k, axis)


def fold(v):
    total = v[0:8]
    for i in range(8, v.shape[0], 8):
        total = total + v[i : i + 8]
    return total


def split(v):
    high = v.astype(BF16)
    return high, (v - high.astype(F32)).astype(BF16)


def picked(weights, v):
    high, low = split(v)
    return nn(weights, high) + nn(weights, low)


def whole_sum(v):
    return jnp.sum(jnp.sum(v, axis=0, keepdims=True), axis=1, keepdims=True)


def kernel(
    n,
    perm_ref,
    storage_ref,
    right_ref,
    coupling_ref,
    gains_ref,
    target_ref,
    column_ref,
    sol_ref,
    res_ref,
    mat,
    coef,
    alpha_ref,
    gamma_ref,
    pivot_ref,
    perm_halo,
    halo_send,
    halo_recv,
    hot_send,
    hot_recv,
    data_send,
    data_recv,
    meta_send,
    meta_recv,
    take_ref,
    give_ref,
    gather_ref,
    scatter_ref,
    gm_ref,
    mat_sem,
    halo_sem,
    hot_sem,
    data_sem,
    meta_sem,
):
    me = lax.axis_index("cells")
    chip = me // 2
    core = me % 2
    chips = n // 2
    along_z = chips // ALONG_Y
    z_here = chip // ALONG_Y
    y_here = chip % ALONG_Y
    sibling = chip * 2 + (1 - core)
    left = lax.rem(me + n - 1, n)
    right = lax.rem(me + 1, n)
    height = coef.shape[1]
    half = height // 2
    comp = target_ref.shape[1]
    slots = chips * 8
    steps = alpha_ref.shape[0]

    load = pltpu.make_async_copy(coupling_ref, mat, mat_sem)
    load.start()

    def greet(device):
        pl.semaphore_signal(
            pltpu.get_barrier_semaphore(),
            inc=1,
            device_id={"cells": device},
            device_id_type=pl.DeviceIdType.MESH,
        )

    def send(src, dst, sems, device):
        copy = pltpu.make_async_remote_copy(
            src_ref=src,
            dst_ref=dst,
            send_sem=sems.at[0],
            recv_sem=sems.at[1],
            device_id={"cells": device},
            device_id_type=pl.DeviceIdType.MESH,
        )
        copy.start()
        return copy

    def await_bytes(ref, sem):
        pltpu.make_async_copy(ref, ref, sem).wait()

    def to_chips(act):
        def plane(j, carry):
            away = along_z // 2 + (j % 2) * (j // 2) - (1 - j % 2) * (j // 2)
            z = lax.rem(z_here + away, along_z)
            for across in (2, 1, 3, 0):
                act(z * ALONG_Y + lax.rem(y_here + across, ALONG_Y))
            return carry

        lax.fori_loop(1, along_z, plane, 0)
        for across in (2, 1, 3):
            act(z_here * ALONG_Y + lax.rem(y_here + across, ALONG_Y))

    to_chips(lambda q: greet(q * 2 + core))
    greet(left)
    greet(right)
    greet(sibling)

    lane = iota((height, LANES), 1)
    row = iota((height, LANES), 0)
    first_layer = lane < 64
    perm = perm_ref[...].T
    r0 = right_ref[...].T

    t_all = jnp.broadcast_to(target_ref[...].astype(F32), (LANES, LANES))
    c_all = jnp.broadcast_to(column_ref[...].astype(F32), (LANES, LANES))
    t_side = t_all.T
    c_side = c_all.T
    sq_row = iota((LANES, LANES), 0)
    sq_lane = iota((LANES, LANES), 1)
    same = t_all == t_side
    rank_all = jnp.sum(jnp.where(same & (sq_row < sq_lane), 1.0, 0.0), axis=0, keepdims=True)
    rank_side = jnp.sum(jnp.where(same & (sq_lane < sq_row), 1.0, 0.0), axis=1, keepdims=True)

    def parts(target, rank):
        t = target.astype(jnp.int32)
        return lax.shift_right_logical(t, 1), t & 1, rank.astype(jnp.int32)

    q_all, core_all, rank_all = parts(t_all[0:1], rank_all)
    q_side, core_side, rank_side = parts(t_side[:, 0:1], rank_side)
    out_row = q_all * 8 + core_all * 4 + rank_all * 2
    give_ref[...] = jnp.where(
        iota((slots, 2 * comp), 0) == jnp.concatenate([out_row, out_row + 1], axis=1), 1.0, 0.0
    ).astype(BF16)
    in_row = jnp.where(core_side == core, 0, slots) + q_side * 8 + core * 4 + rank_side * 2
    take_ref[...] = jnp.where(
        iota((2 * comp, 2 * slots), 1) == jnp.concatenate([in_row, in_row + 1], axis=0), 1.0, 0.0
    ).astype(BF16)
    weight = jnp.where(core_all == 1, 4.0, 1.0) * jnp.where(rank_all == 1, 2.0, 1.0)
    hot = jnp.where(c_side.astype(jnp.int32) == sq_lane, 1.0, 0.0).astype(BF16)
    codes = nn(jnp.where(iota((chips, comp), 0) == q_all, weight, 0.0).astype(BF16), hot)
    for q in range(chips):
        hot_send[q] = codes[q : q + 1]

    pl.semaphore_wait(pltpu.get_barrier_semaphore(), chips + 2)

    hot_recv[0, pl.ds(chip, 1)] = hot_send[pl.ds(chip, 1)]
    to_chips(lambda q: send(hot_send.at[q], hot_recv.at[0, chip], hot_sem.at[0], q * 2 + core))
    perm_right = send(
        perm_ref.at[pl.ds(64, 64)], perm_halo.at[pl.ds(0, 64)], halo_sem.at[0], right
    )
    perm_left = send(
        perm_ref.at[pl.ds(0, 64)], perm_halo.at[pl.ds(64, 64)], halo_sem.at[1], left
    )

    trans_in = harmonic(perm, up(perm, 64, 1))
    y_low = jnp.where((lane & 63) == 0, 0.0, harmonic(perm, up(perm, 1, 1)))
    y_high = down(y_low, 1, 1)
    z_low = jnp.where(row == 0, 0.0, harmonic(perm, up(perm, 1)))
    z_high = down(z_low, 1)
    coef[1] = trans_in
    coef[3] = y_low
    coef[4] = y_high
    coef[5] = z_low
    coef[6] = z_high
    part_diag = storage_ref[...].T + trans_in + y_low + y_high + z_low + z_high

    perm_right.wait_recv()
    perm_left.wait_recv()
    trans_out = harmonic(perm, perm_halo[...].T)
    outside = (first_layer & (me == 0)) | (jnp.logical_not(first_layer) & (me == n - 1))
    trans_out = jnp.where(outside, 0.0, trans_out)
    coef[2] = trans_out
    coef[0] = part_diag + trans_out

    a = -z_low
    b = coef[0]
    for s in range(steps):
        k = 1 << s
        rb = 1.0 / b
        scaled = -a * rb
        alpha = -a * up(rb, k)
        gamma = down(scaled, k)
        alpha_ref[s] = alpha
        gamma_ref[s] = gamma
        b = b + down(a * scaled, k) + alpha * a
        if s + 1 < steps:
            a = alpha * up(a, k)
    pivot_ref[...] = 1.0 / b

    def precondition(d):
        for s in range(steps):
            k = 1 << s
            d = d + alpha_ref[s] * up(d, k) + gamma_ref[s] * down(d, k)
        return d * pivot_ref[...]

    def start_halo(v, which):
        top, bottom = v[:half], v[half:]
        low = iota(top.shape, 1) < 64
        halo_send[which, 0] = jnp.where(low, up(top, 64, 1), bottom)
        halo_send[which, 1] = jnp.where(low, top, up(bottom, 64, 1))
        return (
            send(
                halo_send.at[which, 0],
                halo_recv.at[which, 0],
                halo_sem.at[2 + 2 * which],
                right,
            ),
            send(
                halo_send.at[which, 1],
                halo_recv.at[which, 1],
                halo_sem.at[3 + 2 * which],
                left,
            ),
        )

    def stencil(v, which, copies):
        part = (
            coef[0] * v
            - coef[1] * up(v, 64, 1)
            - coef[3] * up(v, 1, 1)
            - coef[4] * down(v, 1, 1)
            - coef[5] * up(v, 1)
            - coef[6] * down(v, 1)
        )
        for copy in copies:
            copy.wait_recv()
        before, after = halo_recv[which, 0], halo_recv[which, 1]
        low = iota(before.shape, 1) < 64
        halo = jnp.concatenate(
            [
                jnp.where(low, before, up(after, 64, 1)),
                jnp.where(low, up(before, 64, 1), after),
            ],
            axis=0,
        )
        return part - coef[2] * halo

    def wells(rows):
        chosen = rows.astype(BF16)
        backs, dot = [], jnp.zeros((8, LANES), F32)
        for g in range(comp // GROUP):
            block = mat[pl.ds(g * GROUP * 64, GROUP * 64), :]
            y = nt(chosen[g * GROUP : (g + 1) * GROUP], block)
            u = (y * gm_ref[pl.ds(g * GROUP, GROUP), :]).astype(BF16)
            backs.append(nn(u, block))
            both = fold(y * u.astype(F32))
            for i in range(0, GROUP * 64, LANES):
                dot = dot + both[:, i : i + LANES]
        return jnp.concatenate(backs, axis=0), dot

    def start_exchange(which, v, sums):
        largest = jnp.maximum(jnp.max(jnp.max(jnp.abs(v), axis=0, keepdims=True), axis=1, keepdims=True), 1e-30)
        fixed = jnp.round(v * (LARGEST / largest))
        data_send[which] = fixed.astype(jnp.int32).astype(jnp.int16).reshape(chips, 8, LANES)
        at = iota((1, LANES), 1)
        meta = jnp.where(at == 0, largest * (1.0 / LARGEST), 0.0)
        for i, term in enumerate(sums):
            meta = jnp.where(at == i + 1, whole_sum(term), meta)
        meta_send[which] = meta
        data_recv[which, 0, pl.ds(chip, 1)] = data_send[which, pl.ds(chip, 1)]
        meta_recv[which, 0, pl.ds(chip, 1)] = meta[None]

        def act(q):
            send(data_send.at[which, q], data_recv.at[which, 0, chip], data_sem.at[which, 0], q * 2 + core)
            send(meta_send.at[which], meta_recv.at[which, 0, chip], meta_sem.at[which, 0], q * 2 + core)

        to_chips(act)

    def swap(ref, sems):
        await_bytes(ref.at[0, pl.ds(0, chips - 1)], sems.at[0, 1])
        return send(ref.at[0], ref.at[1], sems.at[1], sibling)

    def finish_exchange(which, weights):
        data = data_recv.at[which]
        meta = meta_recv.at[which]
        data_swap = swap(data, data_sem.at[which])
        meta_swap = swap(meta, meta_sem.at[which])

        def received(side):
            unit = meta[side][:, :, 0:1]
            v = data[side].astype(jnp.int32).astype(F32) * unit
            return picked(weights[:, side * slots : (side + 1) * slots], v.reshape(slots, LANES))

        total = received(0)
        data_swap.wait_recv()
        meta_swap.wait_recv()
        total = total + received(1)
        sums = jnp.sum(meta[0], axis=0) + jnp.sum(meta[1], axis=0)
        return total, sums

    def drain(ref_one, ref_all, sems):
        await_bytes(ref_all.at[0, pl.ds(0, chips - 1)], sems.at[0, 0])
        await_bytes(ref_one.at[0], sems.at[1, 0])

    def columns_of(v):
        return jnp.concatenate([v[:half].T, v[half:].T], axis=0)

    def side_by_side(v):
        return jnp.concatenate([v[:comp], v[comp:]], axis=1)

    def stacked(v):
        return jnp.concatenate([v[:, :half], v[:, half:]], axis=0)

    z0 = precondition(r0)

    hot_swap = swap(hot_recv, hot_sem)
    z0_cols = columns_of(z0)
    z0_high, z0_low = split(z0_cols)
    hot_swap.wait_recv()
    codes = jnp.concatenate([hot_recv[0, :, 0, :], hot_recv[1, :, 0, :]], axis=0).astype(BF16)
    r = iota((slots, 2 * chips), 0)
    source = lax.shift_right_logical(r, 3) + jnp.where(
        (lax.shift_right_logical(r, 2) & 1) == core, 0, chips
    )
    spread = jnp.where(iota((slots, 2 * chips), 1) == source, 1.0, 0.0).astype(BF16)
    r = iota((slots, LANES), 0)
    bit = lax.shift_right_logical(r, 1) & 1
    asked = nn(spread, codes).astype(jnp.int32)
    asked = (lax.shift_right_logical(asked, 2 * core + bit) & 1).astype(F32)
    upper = (r & 1) == 1
    gather_ref[...] = jnp.concatenate(
        [jnp.where(upper, 0.0, asked), jnp.where(upper, asked, 0.0)], axis=1
    ).astype(BF16)
    start_exchange(0, nn(gather_ref[...], z0_high) + nn(gather_ref[...], z0_low), [])
    halo0 = start_halo(z0, 0)

    r = iota((2 * chips, 2 * slots), 1)
    spread = jnp.where(
        lax.shift_right_logical(r, 3) == iota((2 * chips, 2 * slots), 0), 1.0, 0.0
    ).astype(BF16)
    asked = nn(codes.astype(F32).T.astype(BF16), spread).astype(jnp.int32)
    r = iota((LANES, 2 * slots), 1)
    bit = lax.shift_right_logical(r, 1) & 1
    mine = (lax.shift_right_logical(r, 2) & 1) == core
    asked = (lax.shift_right_logical(asked, 2 * core + bit) & 1).astype(F32)
    asked = jnp.where(mine, asked, 0.0)
    upper = (r & 1) == 1
    scatter_ref[...] = jnp.concatenate(
        [jnp.where(upper, 0.0, asked), jnp.where(upper, asked, 0.0)], axis=0
    ).astype(BF16)

    gains = gains_ref[...].astype(F32).T.astype(BF16)
    wide = GROUP * 64
    spread = jnp.where((iota((64, wide), 1) & 63) == iota((64, wide), 0), 1.0, 0.0)
    gm_ref[...] = jnp.where(
        (iota((comp, wide), 0) & (GROUP - 1)) == lax.shift_right_logical(iota((comp, wide), 1), 6),
        nn(gains, spread.astype(BF16)),
        0.0,
    )
    s0 = stencil(z0, 0, halo0)
    rz_part = fold(r0 * z0)
    zs_part = fold(z0 * s0)
    load.wait()

    rows, _ = finish_exchange(0, take_ref)
    rows0 = side_by_side(rows)
    back, yu = wells(rows0)
    start_exchange(1, picked(give_ref[...], stacked(back)), [rz_part, zs_part + yu])
    added, sums = finish_exchange(1, scatter_ref)
    rz0, g00 = sums[:, 1:2], sums[:, 2:3]
    alpha0 = rz0 / g00
    w0 = jnp.concatenate([added[:LANES].T, added[LANES:].T], axis=0)
    r1 = r0 - alpha0 * (s0 + w0)
    z1 = precondition(r1)

    start_exchange(2, picked(gather_ref[...], columns_of(z1)), [fold(r1 * z1)])
    halo1 = start_halo(z1, 1)
    s1 = stencil(z1, 1, halo1)
    rows, sums = finish_exchange(2, take_ref)
    fresh = sums[:, 1:2]
    beta = fresh / rz0
    back, yu = wells(side_by_side(rows) + beta * rows0)
    d1 = z1 + beta * z0
    image = s1 + beta * s0
    start_exchange(3, picked(give_ref[...], stacked(back)), [fold(d1 * image) + yu])
    added, sums = finish_exchange(3, scatter_ref)
    alpha1 = fresh / sums[:, 1:2]
    sol_ref[...] = (alpha0 * z0 + alpha1 * d1).T
    w1 = jnp.concatenate([added[:LANES].T, added[LANES:].T], axis=0)
    res_ref[...] = (r1 - alpha1 * (image + w1)).T

    for copy in (perm_right, perm_left, *halo0, *halo1):
        copy.wait_send()
    drain(hot_recv, hot_recv, hot_sem)
    for i in range(4):
        drain(data_recv.at[i], data_recv.at[i], data_sem.at[i])
        drain(meta_recv.at[i], meta_recv.at[i], meta_sem.at[i])


def on_device(perm, storage, right_side, coupling, gains, well_target, well_column):
    n = lax.axis_size("cells")
    chips = n // 2
    comp, perforations, height = coupling.shape
    slots = chips * 8
    shape = perm.shape
    columns = shape[0] * shape[1]
    steps = (height - 1).bit_length()

    def flat(x):
        return x.reshape(columns, height)

    vmem = pl.BlockSpec(memory_space=pltpu.VMEM)
    dma = pltpu.SemaphoreType.DMA
    sol, res = pl.pallas_call(
        functools.partial(kernel, n),
        out_shape=[jax.ShapeDtypeStruct((columns, height), F32)] * 2,
        in_specs=[vmem] * 3 + [pl.BlockSpec(memory_space=pl.ANY)] + [vmem] * 3,
        out_specs=[vmem] * 2,
        scratch_shapes=[
            pltpu.VMEM((comp * perforations, height), BF16),
            pltpu.VMEM((7, height, LANES), F32),
            pltpu.VMEM((steps, height, LANES), F32),
            pltpu.VMEM((steps, height, LANES), F32),
            pltpu.VMEM((height, LANES), F32),
            pltpu.VMEM((columns, height), F32),
            pltpu.VMEM((2, 2, height // 2, LANES), F32),
            pltpu.VMEM((2, 2, height // 2, LANES), F32),
            pltpu.VMEM((chips, 1, LANES), F32),
            pltpu.VMEM((2, chips, 1, LANES), F32),
            pltpu.VMEM((4, chips, 8, LANES), jnp.int16),
            pltpu.VMEM((4, 2, chips, 8, LANES), jnp.int16),
            pltpu.VMEM((4, 1, LANES), F32),
            pltpu.VMEM((4, 2, chips, 1, LANES), F32),
            pltpu.VMEM((2 * comp, 2 * slots), BF16),
            pltpu.VMEM((slots, 2 * comp), BF16),
            pltpu.VMEM((slots, 2 * LANES), BF16),
            pltpu.VMEM((2 * LANES, 2 * slots), BF16),
            pltpu.VMEM((comp, GROUP * perforations), F32),
            dma,
            dma((6, 2)),
            dma((2, 2)),
            dma((4, 2, 2)),
            dma((4, 2, 2)),
        ],
        compiler_params=pltpu.CompilerParams(
            collective_id=0, has_side_effects=True, vmem_limit_bytes=48 * 1024 * 1024
        ),
    )(
        flat(perm),
        flat(storage),
        flat(right_side),
        coupling.reshape(comp * perforations, height),
        gains.T,
        well_target.reshape(1, comp),
        well_column.reshape(1, comp),
    )
    return sol.reshape(shape), res.reshape(shape)


def solution(mesh):
    cells = P(("shift", "cells"), None, None)
    in_specs = (
        cells,
        cells,
        cells,
        P("cells", None, None),
        P("cells", None),
        P("cells", None),
        P("cells"),
    )
    return jax.shard_map(
        on_device, mesh=mesh, in_specs=in_specs, out_specs=(cells, cells), check_vma=False
    )
```

```python
import functools

import jax
import jax.numpy as jnp
from jax import lax
from jax.experimental import pallas as pl
from jax.experimental.pallas import tpu as pltpu
from jax.sharding import PartitionSpec as P

F32 = jnp.float32
BF16 = jnp.bfloat16
LANES = 128
GROUP = 16
ALONG_Y = 4
LARGEST = 32767.0


def nt(a, b):
    return lax.dot_general(a, b, (((1,), (1,)), ((), ())), preferred_element_type=F32)


def nn(a, b):
    return lax.dot_general(a, b, (((1,), (0,)), ((), ())), preferred_element_type=F32)


def iota(shape, dim):
    return lax.broadcasted_iota(jnp.int32, shape, dim)


def harmonic(first, second):
    return 2.0 * first * second / (first + second)


def up(v, k, axis=0):
    return pltpu.roll(v, k, axis)


def down(v, k, axis=0):
    return pltpu.roll(v, v.shape[axis] - k, axis)


def fold(v):
    total = v[0:8]
    for i in range(8, v.shape[0], 8):
        total = total + v[i : i + 8]
    return total


def split(v):
    high = v.astype(BF16)
    return high, (v - high.astype(F32)).astype(BF16)


def picked(weights, v):
    high, low = split(v)
    return nn(weights, high) + nn(weights, low)


def whole_sum(v):
    return jnp.sum(jnp.sum(v, axis=0, keepdims=True), axis=1, keepdims=True)


def kernel(
    n,
    perm_hbm,
    storage_hbm,
    right_hbm,
    coupling_hbm,
    gains_hbm,
    target_hbm,
    column_hbm,
    sol_ref,
    res_ref,
    perm_ref,
    storage_ref,
    right_ref,
    gains_ref,
    target_ref,
    column_ref,
    mat,
    coef,
    alpha_ref,
    gamma_ref,
    pivot_ref,
    perm_halo,
    halo_send,
    halo_recv,
    hot_send,
    hot_recv,
    data_send,
    data_recv,
    meta_send,
    meta_recv,
    take_ref,
    give_ref,
    gather_ref,
    scatter_ref,
    gm_ref,
    mat_t,
    load_sem,
    halo_sem,
    hot_sem,
    data_sem,
    meta_sem,
):
    me = lax.axis_index("cells")
    chip = me // 2
    core = me % 2
    chips = n // 2
    along_z = chips // ALONG_Y
    z_here = chip // ALONG_Y
    y_here = chip % ALONG_Y
    sibling = chip * 2 + (1 - core)
    left = lax.rem(me + n - 1, n)
    right = lax.rem(me + 1, n)
    height = coef.shape[1]
    half = height // 2
    comp = target_ref.shape[1]
    slots = chips * 8
    steps = alpha_ref.shape[0]

    loads = [
        pltpu.make_async_copy(src, dst, load_sem.at[i])
        for i, (src, dst) in enumerate(
            [
                (target_hbm, target_ref),
                (column_hbm, column_ref),
                (perm_hbm, perm_ref),
                (right_hbm, right_ref),
                (storage_hbm, storage_ref),
                (gains_hbm, gains_ref),
                (coupling_hbm, mat),
            ]
        )
    ]
    for load in loads:
        load.start()

    def greet(device):
        pl.semaphore_signal(
            pltpu.get_barrier_semaphore(),
            inc=1,
            device_id={"cells": device},
            device_id_type=pl.DeviceIdType.MESH,
        )

    def send(src, dst, sems, device):
        copy = pltpu.make_async_remote_copy(
            src_ref=src,
            dst_ref=dst,
            send_sem=sems.at[0],
            recv_sem=sems.at[1],
            device_id={"cells": device},
            device_id_type=pl.DeviceIdType.MESH,
        )
        copy.start()
        return copy

    def await_bytes(ref, sem):
        pltpu.make_async_copy(ref, ref, sem).wait()

    def to_chips(act):
        def plane(j, carry):
            away = along_z // 2 + (j % 2) * (j // 2) - (1 - j % 2) * (j // 2)
            z = lax.rem(z_here + away, along_z)
            for across in (2, 1, 3, 0):
                act(z * ALONG_Y + lax.rem(y_here + across, ALONG_Y))
            return carry

        lax.fori_loop(1, along_z, plane, 0)
        for across in (2, 1, 3):
            act(z_here * ALONG_Y + lax.rem(y_here + across, ALONG_Y))

    to_chips(lambda q: greet(q * 2 + core))
    greet(left)
    greet(right)
    greet(sibling)

    for load in loads[:6]:
        load.wait()
    lane = iota((height, LANES), 1)
    row = iota((height, LANES), 0)
    first_layer = lane < 64
    perm = perm_ref[...].T
    r0 = right_ref[...].T

    t_all = jnp.broadcast_to(target_ref[...].astype(F32), (LANES, LANES))
    c_all = jnp.broadcast_to(column_ref[...].astype(F32), (LANES, LANES))
    t_side = t_all.T
    c_side = c_all.T
    sq_row = iota((LANES, LANES), 0)
    sq_lane = iota((LANES, LANES), 1)
    same = t_all == t_side
    rank_all = jnp.sum(jnp.where(same & (sq_row < sq_lane), 1.0, 0.0), axis=0, keepdims=True)
    rank_side = jnp.sum(jnp.where(same & (sq_lane < sq_row), 1.0, 0.0), axis=1, keepdims=True)

    def parts(target, rank):
        t = target.astype(jnp.int32)
        return lax.shift_right_logical(t, 1), t & 1, rank.astype(jnp.int32)

    q_all, core_all, rank_all = parts(t_all[0:1], rank_all)
    q_side, core_side, rank_side = parts(t_side[:, 0:1], rank_side)
    out_row = q_all * 8 + core_all * 4 + rank_all * 2
    give_ref[...] = jnp.where(
        iota((slots, 2 * comp), 0) == jnp.concatenate([out_row, out_row + 1], axis=1), 1.0, 0.0
    ).astype(BF16)
    in_row = jnp.where(core_side == core, 0, slots) + q_side * 8 + core * 4 + rank_side * 2
    take_ref[...] = jnp.where(
        iota((2 * comp, 2 * slots), 1) == jnp.concatenate([in_row, in_row + 1], axis=0), 1.0, 0.0
    ).astype(BF16)
    weight = jnp.where(core_all == 1, 4.0, 1.0) * jnp.where(rank_all == 1, 2.0, 1.0)
    hot = jnp.where(c_side.astype(jnp.int32) == sq_lane, 1.0, 0.0).astype(BF16)
    codes = nn(jnp.where(iota((chips, comp), 0) == q_all, weight, 0.0).astype(BF16), hot)
    for q in range(chips):
        hot_send[q] = codes[q : q + 1]

    loads[6].wait()
    for g in range(comp // GROUP):
        rows = pl.ds(g * GROUP * 64, GROUP * 64)
        mat_t[:, rows] = mat[rows, :].T

    pl.semaphore_wait(pltpu.get_barrier_semaphore(), chips + 2)

    hot_recv[0, pl.ds(chip, 1)] = hot_send[pl.ds(chip, 1)]
    to_chips(lambda q: send(hot_send.at[q], hot_recv.at[0, chip], hot_sem.at[0], q * 2 + core))
    perm_right = send(
        perm_ref.at[pl.ds(64, 64)], perm_halo.at[pl.ds(0, 64)], halo_sem.at[0], right
    )
    perm_left = send(
        perm_ref.at[pl.ds(0, 64)], perm_halo.at[pl.ds(64, 64)], halo_sem.at[1], left
    )

    trans_in = harmonic(perm, up(perm, 64, 1))
    y_low = jnp.where((lane & 63) == 0, 0.0, harmonic(perm, up(perm, 1, 1)))
    y_high = down(y_low, 1, 1)
    z_low = jnp.where(row == 0, 0.0, harmonic(perm, up(perm, 1)))
    z_high = down(z_low, 1)
    coef[1] = trans_in
    coef[3] = y_low
    coef[4] = y_high
    coef[5] = z_low
    coef[6] = z_high
    part_diag = storage_ref[...].T + trans_in + y_low + y_high + z_low + z_high

    perm_right.wait_recv()
    perm_left.wait_recv()
    trans_out = harmonic(perm, perm_halo[...].T)
    outside = (first_layer & (me == 0)) | (jnp.logical_not(first_layer) & (me == n - 1))
    trans_out = jnp.where(outside, 0.0, trans_out)
    coef[2] = trans_out
    coef[0] = part_diag + trans_out

    a = -z_low
    b = coef[0]
    for s in range(steps):
        k = 1 << s
        rb = 1.0 / b
        scaled = -a * rb
        alpha = -a * up(rb, k)
        gamma = down(scaled, k)
        alpha_ref[s] = alpha
        gamma_ref[s] = gamma
        b = b + down(a * scaled, k) + alpha * a
        if s + 1 < steps:
            a = alpha * up(a, k)
    pivot_ref[...] = 1.0 / b

    def precondition(d):
        for s in range(steps):
            k = 1 << s
            d = d + alpha_ref[s] * up(d, k) + gamma_ref[s] * down(d, k)
        return d * pivot_ref[...]

    def start_halo(v, which):
        top, bottom = v[:half], v[half:]
        low = iota(top.shape, 1) < 64
        halo_send[which, 0] = jnp.where(low, up(top, 64, 1), bottom)
        halo_send[which, 1] = jnp.where(low, top, up(bottom, 64, 1))
        return (
            send(
                halo_send.at[which, 0],
                halo_recv.at[which, 0],
                halo_sem.at[2 + 2 * which],
                right,
            ),
            send(
                halo_send.at[which, 1],
                halo_recv.at[which, 1],
                halo_sem.at[3 + 2 * which],
                left,
            ),
        )

    def stencil(v, which, copies):
        part = (
            coef[0] * v
            - coef[1] * up(v, 64, 1)
            - coef[3] * up(v, 1, 1)
            - coef[4] * down(v, 1, 1)
            - coef[5] * up(v, 1)
            - coef[6] * down(v, 1)
        )
        for copy in copies:
            copy.wait_recv()
        before, after = halo_recv[which, 0], halo_recv[which, 1]
        low = iota(before.shape, 1) < 64
        halo = jnp.concatenate(
            [
                jnp.where(low, before, up(after, 64, 1)),
                jnp.where(low, up(before, 64, 1), after),
            ],
            axis=0,
        )
        return part - coef[2] * halo

    def wells(rows):
        chosen = rows.astype(BF16)
        backs, dot = [], jnp.zeros((8, LANES), F32)
        for g in range(comp // GROUP):
            block = mat[pl.ds(g * GROUP * 64, GROUP * 64), :]
            y = nn(chosen[g * GROUP : (g + 1) * GROUP], mat_t[:, pl.ds(g * GROUP * 64, GROUP * 64)])
            u = (y * gm_ref[pl.ds(g * GROUP, GROUP), :]).astype(BF16)
            backs.append(nn(u, block))
            both = fold(y * u.astype(F32))
            for i in range(0, GROUP * 64, LANES):
                dot = dot + both[:, i : i + LANES]
        return jnp.concatenate(backs, axis=0), dot

    def start_exchange(which, v, sums):
        largest = jnp.maximum(jnp.max(jnp.max(jnp.abs(v), axis=0, keepdims=True), axis=1, keepdims=True), 1e-30)
        fixed = jnp.round(v * (LARGEST / largest))
        data_send[which] = fixed.astype(jnp.int32).astype(jnp.int16).reshape(chips, 8, LANES)
        at = iota((1, LANES), 1)
        meta = jnp.where(at == 0, largest * (1.0 / LARGEST), 0.0)
        for i, term in enumerate(sums):
            meta = jnp.where(at == i + 1, whole_sum(term), meta)
        meta_send[which] = meta
        data_recv[which, 0, pl.ds(chip, 1)] = data_send[which, pl.ds(chip, 1)]
        meta_recv[which, 0, pl.ds(chip, 1)] = meta[None]

        def act(q):
            send(data_send.at[which, q], data_recv.at[which, 0, chip], data_sem.at[which, 0], q * 2 + core)
            send(meta_send.at[which], meta_recv.at[which, 0, chip], meta_sem.at[which, 0], q * 2 + core)

        to_chips(act)

    def swap(ref, sems):
        await_bytes(ref.at[0, pl.ds(0, chips - 1)], sems.at[0, 1])
        return send(ref.at[0], ref.at[1], sems.at[1], sibling)

    def finish_exchange(which, weights):
        data = data_recv.at[which]
        meta = meta_recv.at[which]
        data_swap = swap(data, data_sem.at[which])
        meta_swap = swap(meta, meta_sem.at[which])

        def received(side):
            unit = meta[side][:, :, 0:1]
            v = data[side].astype(jnp.int32).astype(F32) * unit
            return picked(weights[:, side * slots : (side + 1) * slots], v.reshape(slots, LANES))

        total = received(0)
        data_swap.wait_recv()
        meta_swap.wait_recv()
        total = total + received(1)
        sums = jnp.sum(meta[0], axis=0) + jnp.sum(meta[1], axis=0)
        return total, sums

    def drain(ref_one, ref_all, sems):
        await_bytes(ref_all.at[0, pl.ds(0, chips - 1)], sems.at[0, 0])
        await_bytes(ref_one.at[0], sems.at[1, 0])

    def columns_of(v):
        return jnp.concatenate([v[:half].T, v[half:].T], axis=0)

    def side_by_side(v):
        return jnp.concatenate([v[:comp], v[comp:]], axis=1)

    def stacked(v):
        return jnp.concatenate([v[:, :half], v[:, half:]], axis=0)

    z0 = precondition(r0)

    hot_swap = swap(hot_recv, hot_sem)
    z0_cols = columns_of(z0)
    z0_high, z0_low = split(z0_cols)
    hot_swap.wait_recv()
    codes = jnp.concatenate([hot_recv[0, :, 0, :], hot_recv[1, :, 0, :]], axis=0).astype(BF16)
    r = iota((slots, 2 * chips), 0)
    source = lax.shift_right_logical(r, 3) + jnp.where(
        (lax.shift_right_logical(r, 2) & 1) == core, 0, chips
    )
    spread = jnp.where(iota((slots, 2 * chips), 1) == source, 1.0, 0.0).astype(BF16)
    r = iota((slots, LANES), 0)
    bit = lax.shift_right_logical(r, 1) & 1
    asked = nn(spread, codes).astype(jnp.int32)
    asked = (lax.shift_right_logical(asked, 2 * core + bit) & 1).astype(F32)
    upper = (r & 1) == 1
    gather_ref[...] = jnp.concatenate(
        [jnp.where(upper, 0.0, asked), jnp.where(upper, asked, 0.0)], axis=1
    ).astype(BF16)
    start_exchange(0, nn(gather_ref[...], z0_high) + nn(gather_ref[...], z0_low), [])
    halo0 = start_halo(z0, 0)

    r = iota((2 * chips, 2 * slots), 1)
    spread = jnp.where(
        lax.shift_right_logical(r, 3) == iota((2 * chips, 2 * slots), 0), 1.0, 0.0
    ).astype(BF16)
    asked = nn(codes.astype(F32).T.astype(BF16), spread).astype(jnp.int32)
    r = iota((LANES, 2 * slots), 1)
    bit = lax.shift_right_logical(r, 1) & 1
    mine = (lax.shift_right_logical(r, 2) & 1) == core
    asked = (lax.shift_right_logical(asked, 2 * core + bit) & 1).astype(F32)
    asked = jnp.where(mine, asked, 0.0)
    upper = (r & 1) == 1
    scatter_ref[...] = jnp.concatenate(
        [jnp.where(upper, 0.0, asked), jnp.where(upper, asked, 0.0)], axis=0
    ).astype(BF16)

    gains = gains_ref[...].astype(F32).T.astype(BF16)
    wide = GROUP * 64
    spread = jnp.where((iota((64, wide), 1) & 63) == iota((64, wide), 0), 1.0, 0.0)
    gm_ref[...] = jnp.where(
        (iota((comp, wide), 0) & (GROUP - 1)) == lax.shift_right_logical(iota((comp, wide), 1), 6),
        nn(gains, spread.astype(BF16)),
        0.0,
    )
    s0 = stencil(z0, 0, halo0)
    rz_part = fold(r0 * z0)
    zs_part = fold(z0 * s0)
    rows, _ = finish_exchange(0, take_ref)
    rows0 = side_by_side(rows)
    back, yu = wells(rows0)
    start_exchange(1, picked(give_ref[...], stacked(back)), [rz_part, zs_part + yu])
    added, sums = finish_exchange(1, scatter_ref)
    rz0, g00 = sums[:, 1:2], sums[:, 2:3]
    alpha0 = rz0 / g00
    w0 = jnp.concatenate([added[:LANES].T, added[LANES:].T], axis=0)
    r1 = r0 - alpha0 * (s0 + w0)
    z1 = precondition(r1)

    start_exchange(2, picked(gather_ref[...], columns_of(z1)), [fold(r1 * z1)])
    halo1 = start_halo(z1, 1)
    s1 = stencil(z1, 1, halo1)
    rows, sums = finish_exchange(2, take_ref)
    fresh = sums[:, 1:2]
    beta = fresh / rz0
    back, yu = wells(side_by_side(rows) + beta * rows0)
    d1 = z1 + beta * z0
    image = s1 + beta * s0
    start_exchange(3, picked(give_ref[...], stacked(back)), [fold(d1 * image) + yu])
    added, sums = finish_exchange(3, scatter_ref)
    alpha1 = fresh / sums[:, 1:2]
    sol_ref[...] = (alpha0 * z0 + alpha1 * d1).T
    w1 = jnp.concatenate([added[:LANES].T, added[LANES:].T], axis=0)
    res_ref[...] = (r1 - alpha1 * (image + w1)).T

    for copy in (perm_right, perm_left, *halo0, *halo1):
        copy.wait_send()
    drain(hot_recv, hot_recv, hot_sem)
    for i in range(4):
        drain(data_recv.at[i], data_recv.at[i], data_sem.at[i])
        drain(meta_recv.at[i], meta_recv.at[i], meta_sem.at[i])


def on_device(perm, storage, right_side, coupling, gains, well_target, well_column):
    n = lax.axis_size("cells")
    chips = n // 2
    comp, perforations, height = coupling.shape
    slots = chips * 8
    shape = perm.shape
    columns = shape[0] * shape[1]
    steps = (height - 1).bit_length()

    def flat(x):
        return x.reshape(columns, height)

    vmem = pl.BlockSpec(memory_space=pltpu.VMEM)
    dma = pltpu.SemaphoreType.DMA
    sol, res = pl.pallas_call(
        functools.partial(kernel, n),
        out_shape=[jax.ShapeDtypeStruct((columns, height), F32)] * 2,
        in_specs=[pl.BlockSpec(memory_space=pl.ANY)] * 7,
        out_specs=[vmem] * 2,
        scratch_shapes=[
            pltpu.VMEM((columns, height), F32),
            pltpu.VMEM((columns, height), F32),
            pltpu.VMEM((columns, height), F32),
            pltpu.VMEM((perforations, comp), BF16),
            pltpu.VMEM((1, comp), jnp.int32),
            pltpu.VMEM((1, comp), jnp.int32),
            pltpu.VMEM((comp * perforations, height), BF16),
            pltpu.VMEM((7, height, LANES), F32),
            pltpu.VMEM((steps, height, LANES), F32),
            pltpu.VMEM((steps, height, LANES), F32),
            pltpu.VMEM((height, LANES), F32),
            pltpu.VMEM((columns, height), F32),
            pltpu.VMEM((2, 2, height // 2, LANES), F32),
            pltpu.VMEM((2, 2, height // 2, LANES), F32),
            pltpu.VMEM((chips, 1, LANES), F32),
            pltpu.VMEM((2, chips, 1, LANES), F32),
            pltpu.VMEM((4, chips, 8, LANES), jnp.int16),
            pltpu.VMEM((4, 2, chips, 8, LANES), jnp.int16),
            pltpu.VMEM((4, 1, LANES), F32),
            pltpu.VMEM((4, 2, chips, 1, LANES), F32),
            pltpu.VMEM((2 * comp, 2 * slots), BF16),
            pltpu.VMEM((slots, 2 * comp), BF16),
            pltpu.VMEM((slots, 2 * LANES), BF16),
            pltpu.VMEM((2 * LANES, 2 * slots), BF16),
            pltpu.VMEM((comp, GROUP * perforations), F32),
            pltpu.VMEM((height, comp * perforations), BF16),
            dma((7,)),
            dma((6, 2)),
            dma((2, 2)),
            dma((4, 2, 2)),
            dma((4, 2, 2)),
        ],
        compiler_params=pltpu.CompilerParams(
            collective_id=0, has_side_effects=True, vmem_limit_bytes=60 * 1024 * 1024
        ),
    )(
        flat(perm),
        flat(storage),
        flat(right_side),
        coupling.reshape(comp * perforations, height),
        gains.T,
        well_target.reshape(1, comp),
        well_column.reshape(1, comp),
    )
    return sol.reshape(shape), res.reshape(shape)


def solution(mesh):
    cells = P(("shift", "cells"), None, None)
    in_specs = (
        cells,
        cells,
        cells,
        P("cells", None, None),
        P("cells", None),
        P("cells", None),
        P("cells"),
    )
    return jax.shard_map(
        on_device, mesh=mesh, in_specs=in_specs, out_specs=(cells, cells), check_vma=False
    )
```

```python
import functools

import jax
import jax.numpy as jnp
from jax import lax
from jax.experimental import pallas as pl
from jax.experimental.pallas import tpu as pltpu
from jax.sharding import PartitionSpec as P

F32 = jnp.float32
BF16 = jnp.bfloat16
LANES = 128
GROUP = 16
ALONG_Y = 4
LARGEST = 32767.0


def nt(a, b):
    return lax.dot_general(a, b, (((1,), (1,)), ((), ())), preferred_element_type=F32)


def nn(a, b):
    return lax.dot_general(a, b, (((1,), (0,)), ((), ())), preferred_element_type=F32)


def iota(shape, dim):
    return lax.broadcasted_iota(jnp.int32, shape, dim)


def harmonic(first, second):
    return 2.0 * first * second / (first + second)


def up(v, k, axis=0):
    return pltpu.roll(v, k, axis)


def down(v, k, axis=0):
    return pltpu.roll(v, v.shape[axis] - k, axis)


def fold(v):
    total = v[0:8]
    for i in range(8, v.shape[0], 8):
        total = total + v[i : i + 8]
    return total


def split(v):
    high = v.astype(BF16)
    return high, (v - high.astype(F32)).astype(BF16)


def picked(weights, v):
    high, low = split(v)
    return nn(weights, high) + nn(weights, low)


def whole_sum(v):
    return jnp.sum(jnp.sum(v, axis=0, keepdims=True), axis=1, keepdims=True)


def kernel(
    n,
    perm_hbm,
    storage_hbm,
    right_hbm,
    coupling_hbm,
    gains_hbm,
    target_hbm,
    column_hbm,
    sol_ref,
    res_ref,
    perm_ref,
    storage_ref,
    right_ref,
    gains_ref,
    target_ref,
    column_ref,
    mat,
    coef,
    alpha_ref,
    gamma_ref,
    pivot_ref,
    perm_halo,
    halo_send,
    halo_recv,
    hot_send,
    hot_recv,
    rows_send,
    rows_recv,
    data_send,
    data_recv,
    meta_send,
    meta_recv,
    take_ref,
    give_ref,
    gather_ref,
    scatter_ref,
    gm_ref,
    mat_t,
    load_sem,
    halo_sem,
    hot_sem,
    rows_sem,
    data_sem,
    meta_sem,
):
    me = lax.axis_index("cells")
    chip = me // 2
    core = me % 2
    chips = n // 2
    along_z = chips // ALONG_Y
    z_here = chip // ALONG_Y
    y_here = chip % ALONG_Y
    sibling = chip * 2 + (1 - core)
    left = lax.rem(me + n - 1, n)
    right = lax.rem(me + 1, n)
    height = coef.shape[1]
    half = height // 2
    comp = target_ref.shape[1]
    slots = chips * 8
    steps = alpha_ref.shape[0]

    loads = [
        pltpu.make_async_copy(src, dst, load_sem.at[i])
        for i, (src, dst) in enumerate(
            [
                (target_hbm, target_ref),
                (column_hbm, column_ref),
                (perm_hbm, perm_ref),
                (right_hbm, right_ref),
                (storage_hbm, storage_ref),
                (gains_hbm, gains_ref),
                (coupling_hbm, mat),
            ]
        )
    ]
    for load in loads:
        load.start()

    def greet(device):
        pl.semaphore_signal(
            pltpu.get_barrier_semaphore(),
            inc=1,
            device_id={"cells": device},
            device_id_type=pl.DeviceIdType.MESH,
        )

    def send(src, dst, sems, device):
        copy = pltpu.make_async_remote_copy(
            src_ref=src,
            dst_ref=dst,
            send_sem=sems.at[0],
            recv_sem=sems.at[1],
            device_id={"cells": device},
            device_id_type=pl.DeviceIdType.MESH,
        )
        copy.start()
        return copy

    def await_bytes(ref, sem):
        pltpu.make_async_copy(ref, ref, sem).wait()

    def to_chips(act):
        def plane(j, carry):
            away = along_z // 2 + (j % 2) * (j // 2) - (1 - j % 2) * (j // 2)
            z = lax.rem(z_here + away, along_z)
            for across in (2, 1, 3, 0):
                act(z * ALONG_Y + lax.rem(y_here + across, ALONG_Y))
            return carry

        lax.fori_loop(1, along_z, plane, 0)
        for across in (2, 1, 3):
            act(z_here * ALONG_Y + lax.rem(y_here + across, ALONG_Y))

    to_chips(lambda q: greet(q * 2 + core))
    greet(left)
    greet(right)
    greet(sibling)

    for load in loads[:6]:
        load.wait()
    lane = iota((height, LANES), 1)
    row = iota((height, LANES), 0)
    first_layer = lane < 64
    perm = perm_ref[...].T
    r0 = right_ref[...].T

    t_all = jnp.broadcast_to(target_ref[...].astype(F32), (LANES, LANES))
    c_all = jnp.broadcast_to(column_ref[...].astype(F32), (LANES, LANES))
    t_side = t_all.T
    c_side = c_all.T
    sq_row = iota((LANES, LANES), 0)
    sq_lane = iota((LANES, LANES), 1)
    same = t_all == t_side
    rank_all = jnp.sum(jnp.where(same & (sq_row < sq_lane), 1.0, 0.0), axis=0, keepdims=True)
    rank_side = jnp.sum(jnp.where(same & (sq_lane < sq_row), 1.0, 0.0), axis=1, keepdims=True)

    def parts(target, rank):
        t = target.astype(jnp.int32)
        return lax.shift_right_logical(t, 1), t & 1, rank.astype(jnp.int32)

    q_all, core_all, rank_all = parts(t_all[0:1], rank_all)
    q_side, core_side, rank_side = parts(t_side[:, 0:1], rank_side)
    out_row = q_all * 8 + core_all * 4 + rank_all * 2
    give_ref[...] = jnp.where(
        iota((slots, 2 * comp), 0) == jnp.concatenate([out_row, out_row + 1], axis=1), 1.0, 0.0
    ).astype(BF16)
    in_row = jnp.where(core_side == core, 0, slots) + q_side * 8 + core * 4 + rank_side * 2
    take_ref[...] = jnp.where(
        iota((2 * comp, 2 * slots), 1) == jnp.concatenate([in_row, in_row + 1], axis=0), 1.0, 0.0
    ).astype(BF16)
    weight = jnp.where(core_all == 1, 4.0, 1.0) * jnp.where(rank_all == 1, 2.0, 1.0)
    hot = jnp.where(c_side.astype(jnp.int32) == sq_lane, 1.0, 0.0).astype(BF16)
    codes = nn(jnp.where(iota((chips, comp), 0) == q_all, weight, 0.0).astype(BF16), hot)
    for q in range(chips):
        hot_send[q] = codes[q : q + 1]

    loads[6].wait()
    for g in range(comp // GROUP):
        rows = pl.ds(g * GROUP * 64, GROUP * 64)
        mat_t[:, rows] = mat[rows, :].T

    pl.semaphore_wait(pltpu.get_barrier_semaphore(), chips + 2)

    hot_recv[0, pl.ds(chip, 1)] = hot_send[pl.ds(chip, 1)]
    to_chips(lambda q: send(hot_send.at[q], hot_recv.at[0, chip], hot_sem.at[0], q * 2 + core))
    perm_right = send(
        perm_ref.at[pl.ds(64, 64)], perm_halo.at[pl.ds(0, 64)], halo_sem.at[0], right
    )
    perm_left = send(
        perm_ref.at[pl.ds(0, 64)], perm_halo.at[pl.ds(64, 64)], halo_sem.at[1], left
    )

    trans_in = harmonic(perm, up(perm, 64, 1))
    y_low = jnp.where((lane & 63) == 0, 0.0, harmonic(perm, up(perm, 1, 1)))
    y_high = down(y_low, 1, 1)
    z_low = jnp.where(row == 0, 0.0, harmonic(perm, up(perm, 1)))
    z_high = down(z_low, 1)
    coef[1] = trans_in
    coef[3] = y_low
    coef[4] = y_high
    coef[5] = z_low
    coef[6] = z_high
    part_diag = storage_ref[...].T + trans_in + y_low + y_high + z_low + z_high

    perm_right.wait_recv()
    perm_left.wait_recv()
    trans_out = harmonic(perm, perm_halo[...].T)
    outside = (first_layer & (me == 0)) | (jnp.logical_not(first_layer) & (me == n - 1))
    trans_out = jnp.where(outside, 0.0, trans_out)
    coef[2] = trans_out
    coef[0] = part_diag + trans_out

    a = -z_low
    b = coef[0]
    for s in range(steps):
        k = 1 << s
        rb = 1.0 / b
        scaled = -a * rb
        alpha = -a * up(rb, k)
        gamma = down(scaled, k)
        alpha_ref[s] = alpha
        gamma_ref[s] = gamma
        b = b + down(a * scaled, k) + alpha * a
        if s + 1 < steps:
            a = alpha * up(a, k)
    pivot_ref[...] = 1.0 / b

    def precondition(d):
        for s in range(steps):
            k = 1 << s
            d = d + alpha_ref[s] * up(d, k) + gamma_ref[s] * down(d, k)
        return d * pivot_ref[...]

    def start_halo(v, which):
        top, bottom = v[:half], v[half:]
        low = iota(top.shape, 1) < 64
        halo_send[which, 0] = jnp.where(low, up(top, 64, 1), bottom)
        halo_send[which, 1] = jnp.where(low, top, up(bottom, 64, 1))
        return (
            send(
                halo_send.at[which, 0],
                halo_recv.at[which, 0],
                halo_sem.at[2 + 2 * which],
                right,
            ),
            send(
                halo_send.at[which, 1],
                halo_recv.at[which, 1],
                halo_sem.at[3 + 2 * which],
                left,
            ),
        )

    def stencil(v, which, copies):
        part = (
            coef[0] * v
            - coef[1] * up(v, 64, 1)
            - coef[3] * up(v, 1, 1)
            - coef[4] * down(v, 1, 1)
            - coef[5] * up(v, 1)
            - coef[6] * down(v, 1)
        )
        for copy in copies:
            copy.wait_recv()
        before, after = halo_recv[which, 0], halo_recv[which, 1]
        low = iota(before.shape, 1) < 64
        halo = jnp.concatenate(
            [
                jnp.where(low, before, up(after, 64, 1)),
                jnp.where(low, up(before, 64, 1), after),
            ],
            axis=0,
        )
        return part - coef[2] * halo

    def wells(rows):
        chosen = rows.astype(BF16)
        backs, dot = [], jnp.zeros((8, LANES), F32)
        for g in range(comp // GROUP):
            block = mat[pl.ds(g * GROUP * 64, GROUP * 64), :]
            y = nn(chosen[g * GROUP : (g + 1) * GROUP], mat_t[:, pl.ds(g * GROUP * 64, GROUP * 64)])
            u = (y * gm_ref[pl.ds(g * GROUP, GROUP), :]).astype(BF16)
            backs.append(nn(u, block))
            both = fold(y * u.astype(F32))
            for i in range(0, GROUP * 64, LANES):
                dot = dot + both[:, i : i + LANES]
        return jnp.concatenate(backs, axis=0), dot

    def start_rows(which, v):
        rows_send[which] = v.astype(BF16).reshape(chips, 8, LANES)
        rows_recv[which, 0, pl.ds(chip, 1)] = rows_send[which, pl.ds(chip, 1)]
        to_chips(
            lambda q: send(
                rows_send.at[which, q],
                rows_recv.at[which, 0, chip],
                rows_sem.at[which, 0],
                q * 2 + core,
            )
        )

    def finish_rows(which):
        copy = swap(rows_recv.at[which], rows_sem.at[which])
        total = nn(take_ref[:, :slots], rows_recv[which, 0].reshape(slots, LANES))
        copy.wait_recv()
        return total + nn(take_ref[:, slots:], rows_recv[which, 1].reshape(slots, LANES))

    def start_exchange(which, v, sums):
        largest = jnp.maximum(jnp.max(jnp.max(jnp.abs(v), axis=0, keepdims=True), axis=1, keepdims=True), 1e-30)
        fixed = jnp.round(v * (LARGEST / largest))
        data_send[which] = fixed.astype(jnp.int32).astype(jnp.int16).reshape(chips, 8, LANES)
        at = iota((1, LANES), 1)
        meta = jnp.where(at == 0, largest * (1.0 / LARGEST), 0.0)
        for i, term in enumerate(sums):
            meta = jnp.where(at == i + 1, whole_sum(term), meta)
        meta_send[which] = meta
        data_recv[which, 0, pl.ds(chip, 1)] = data_send[which, pl.ds(chip, 1)]
        meta_recv[which, 0, pl.ds(chip, 1)] = meta[None]

        def act(q):
            send(data_send.at[which, q], data_recv.at[which, 0, chip], data_sem.at[which, 0], q * 2 + core)
            send(meta_send.at[which], meta_recv.at[which, 0, chip], meta_sem.at[which, 0], q * 2 + core)

        to_chips(act)

    def swap(ref, sems):
        await_bytes(ref.at[0, pl.ds(0, chips - 1)], sems.at[0, 1])
        return send(ref.at[0], ref.at[1], sems.at[1], sibling)

    def finish_exchange(which):
        weights = scatter_ref
        data = data_recv.at[which]
        meta = meta_recv.at[which]
        data_swap = swap(data, data_sem.at[which])
        meta_swap = swap(meta, meta_sem.at[which])

        def received(side):
            unit = meta[side][:, :, 0:1]
            v = data[side].astype(jnp.int32).astype(F32) * unit
            return picked(weights[:, side * slots : (side + 1) * slots], v.reshape(slots, LANES))

        total = received(0)
        data_swap.wait_recv()
        meta_swap.wait_recv()
        total = total + received(1)
        sums = jnp.sum(meta[0], axis=0) + jnp.sum(meta[1], axis=0)
        return total, sums

    def drain(ref_one, ref_all, sems):
        await_bytes(ref_all.at[0, pl.ds(0, chips - 1)], sems.at[0, 0])
        await_bytes(ref_one.at[0], sems.at[1, 0])

    def columns_of(v):
        return jnp.concatenate([v[:half].T, v[half:].T], axis=0)

    def side_by_side(v):
        return jnp.concatenate([v[:comp], v[comp:]], axis=1)

    def stacked(v):
        return jnp.concatenate([v[:, :half], v[:, half:]], axis=0)

    z0 = precondition(r0)

    hot_swap = swap(hot_recv, hot_sem)
    z0_cols = columns_of(z0).astype(BF16)
    hot_swap.wait_recv()
    codes = jnp.concatenate([hot_recv[0, :, 0, :], hot_recv[1, :, 0, :]], axis=0).astype(BF16)
    r = iota((slots, 2 * chips), 0)
    source = lax.shift_right_logical(r, 3) + jnp.where(
        (lax.shift_right_logical(r, 2) & 1) == core, 0, chips
    )
    spread = jnp.where(iota((slots, 2 * chips), 1) == source, 1.0, 0.0).astype(BF16)
    r = iota((slots, LANES), 0)
    bit = lax.shift_right_logical(r, 1) & 1
    asked = nn(spread, codes).astype(jnp.int32)
    asked = (lax.shift_right_logical(asked, 2 * core + bit) & 1).astype(F32)
    upper = (r & 1) == 1
    gather_ref[...] = jnp.concatenate(
        [jnp.where(upper, 0.0, asked), jnp.where(upper, asked, 0.0)], axis=1
    ).astype(BF16)
    start_rows(0, nn(gather_ref[...], z0_cols))
    halo0 = start_halo(z0, 0)

    r = iota((2 * chips, 2 * slots), 1)
    spread = jnp.where(
        lax.shift_right_logical(r, 3) == iota((2 * chips, 2 * slots), 0), 1.0, 0.0
    ).astype(BF16)
    asked = nn(codes.astype(F32).T.astype(BF16), spread).astype(jnp.int32)
    r = iota((LANES, 2 * slots), 1)
    bit = lax.shift_right_logical(r, 1) & 1
    mine = (lax.shift_right_logical(r, 2) & 1) == core
    asked = (lax.shift_right_logical(asked, 2 * core + bit) & 1).astype(F32)
    asked = jnp.where(mine, asked, 0.0)
    upper = (r & 1) == 1
    scatter_ref[...] = jnp.concatenate(
        [jnp.where(upper, 0.0, asked), jnp.where(upper, asked, 0.0)], axis=0
    ).astype(BF16)

    gains = gains_ref[...].astype(F32).T.astype(BF16)
    wide = GROUP * 64
    spread = jnp.where((iota((64, wide), 1) & 63) == iota((64, wide), 0), 1.0, 0.0)
    gm_ref[...] = jnp.where(
        (iota((comp, wide), 0) & (GROUP - 1)) == lax.shift_right_logical(iota((comp, wide), 1), 6),
        nn(gains, spread.astype(BF16)),
        0.0,
    )
    s0 = stencil(z0, 0, halo0)
    rz_part = fold(r0 * z0)
    zs_part = fold(z0 * s0)
    back, yu = wells(side_by_side(finish_rows(0)))
    start_exchange(0, picked(give_ref[...], stacked(back)), [rz_part, zs_part + yu])
    added, sums = finish_exchange(0)
    rz0, g00 = sums[:, 1:2], sums[:, 2:3]
    alpha0 = rz0 / g00
    w0 = jnp.concatenate([added[:LANES].T, added[LANES:].T], axis=0)
    q0 = s0 + w0
    r1 = r0 - alpha0 * q0
    z1 = precondition(r1)

    start_rows(1, nn(gather_ref[...], columns_of(z1).astype(BF16)))
    halo1 = start_halo(z1, 1)
    s1 = stencil(z1, 1, halo1)
    fresh_part = fold(r1 * z1)
    zq_part = fold(z1 * q0)
    zs_part = fold(z1 * s1)
    back, yu = wells(side_by_side(finish_rows(1)))
    start_exchange(1, picked(give_ref[...], stacked(back)), [fresh_part, zs_part + yu, zq_part])
    added, sums = finish_exchange(1)
    fresh = sums[:, 1:2]
    beta = fresh / rz0
    alpha1 = fresh / (sums[:, 2:3] + 2.0 * beta * sums[:, 3:4] + beta * beta * g00)
    sol_ref[...] = (alpha0 * z0 + alpha1 * (z1 + beta * z0)).T
    w1 = jnp.concatenate([added[:LANES].T, added[LANES:].T], axis=0)
    res_ref[...] = (r1 - alpha1 * (s1 + beta * q0 + w1)).T

    for copy in (perm_right, perm_left, *halo0, *halo1):
        copy.wait_send()
    drain(hot_recv, hot_recv, hot_sem)
    for i in range(2):
        drain(rows_recv.at[i], rows_recv.at[i], rows_sem.at[i])
        drain(data_recv.at[i], data_recv.at[i], data_sem.at[i])
        drain(meta_recv.at[i], meta_recv.at[i], meta_sem.at[i])


def on_device(perm, storage, right_side, coupling, gains, well_target, well_column):
    n = lax.axis_size("cells")
    chips = n // 2
    comp, perforations, height = coupling.shape
    slots = chips * 8
    shape = perm.shape
    columns = shape[0] * shape[1]
    steps = (height - 1).bit_length()

    def flat(x):
        return x.reshape(columns, height)

    vmem = pl.BlockSpec(memory_space=pltpu.VMEM)
    dma = pltpu.SemaphoreType.DMA
    sol, res = pl.pallas_call(
        functools.partial(kernel, n),
        out_shape=[jax.ShapeDtypeStruct((columns, height), F32)] * 2,
        in_specs=[pl.BlockSpec(memory_space=pl.ANY)] * 7,
        out_specs=[vmem] * 2,
        scratch_shapes=[
            pltpu.VMEM((columns, height), F32),
            pltpu.VMEM((columns, height), F32),
            pltpu.VMEM((columns, height), F32),
            pltpu.VMEM((perforations, comp), BF16),
            pltpu.VMEM((1, comp), jnp.int32),
            pltpu.VMEM((1, comp), jnp.int32),
            pltpu.VMEM((comp * perforations, height), BF16),
            pltpu.VMEM((7, height, LANES), F32),
            pltpu.VMEM((steps, height, LANES), F32),
            pltpu.VMEM((steps, height, LANES), F32),
            pltpu.VMEM((height, LANES), F32),
            pltpu.VMEM((columns, height), F32),
            pltpu.VMEM((2, 2, height // 2, LANES), F32),
            pltpu.VMEM((2, 2, height // 2, LANES), F32),
            pltpu.VMEM((chips, 1, LANES), F32),
            pltpu.VMEM((2, chips, 1, LANES), F32),
            pltpu.VMEM((2, chips, 8, LANES), BF16),
            pltpu.VMEM((2, 2, chips, 8, LANES), BF16),
            pltpu.VMEM((2, chips, 8, LANES), jnp.int16),
            pltpu.VMEM((2, 2, chips, 8, LANES), jnp.int16),
            pltpu.VMEM((2, 1, LANES), F32),
            pltpu.VMEM((2, 2, chips, 1, LANES), F32),
            pltpu.VMEM((2 * comp, 2 * slots), BF16),
            pltpu.VMEM((slots, 2 * comp), BF16),
            pltpu.VMEM((slots, 2 * LANES), BF16),
            pltpu.VMEM((2 * LANES, 2 * slots), BF16),
            pltpu.VMEM((comp, GROUP * perforations), F32),
            pltpu.VMEM((height, comp * perforations), BF16),
            dma((7,)),
            dma((6, 2)),
            dma((2, 2)),
            dma((2, 2, 2)),
            dma((2, 2, 2)),
            dma((2, 2, 2)),
        ],
        compiler_params=pltpu.CompilerParams(
            collective_id=0, has_side_effects=True, vmem_limit_bytes=60 * 1024 * 1024
        ),
    )(
        flat(perm),
        flat(storage),
        flat(right_side),
        coupling.reshape(comp * perforations, height),
        gains.T,
        well_target.reshape(1, comp),
        well_column.reshape(1, comp),
    )
    return sol.reshape(shape), res.reshape(shape)


def solution(mesh):
    cells = P(("shift", "cells"), None, None)
    in_specs = (
        cells,
        cells,
        cells,
        P("cells", None, None),
        P("cells", None),
        P("cells", None),
        P("cells"),
    )
    return jax.shard_map(
        on_device, mesh=mesh, in_specs=in_specs, out_specs=(cells, cells), check_vma=False
    )
```

```python
import functools

import jax
import jax.numpy as jnp
from jax import lax
from jax.experimental import pallas as pl
from jax.experimental.pallas import tpu as pltpu
from jax.sharding import PartitionSpec as P

F32 = jnp.float32
BF16 = jnp.bfloat16
LANES = 128
GROUP = 16
ALONG_Y = 4
LARGEST = 32767.0


def nt(a, b):
    return lax.dot_general(a, b, (((1,), (1,)), ((), ())), preferred_element_type=F32)


def nn(a, b):
    return lax.dot_general(a, b, (((1,), (0,)), ((), ())), preferred_element_type=F32)


def iota(shape, dim):
    return lax.broadcasted_iota(jnp.int32, shape, dim)


def harmonic(first, second):
    return 2.0 * first * second / (first + second)


def up(v, k, axis=0):
    return pltpu.roll(v, k, axis)


def down(v, k, axis=0):
    return pltpu.roll(v, v.shape[axis] - k, axis)


def fold(v):
    total = v[0:8]
    for i in range(8, v.shape[0], 8):
        total = total + v[i : i + 8]
    return total


def split(v):
    high = v.astype(BF16)
    return high, (v - high.astype(F32)).astype(BF16)


def picked(weights, v):
    high, low = split(v)
    return nn(weights, high) + nn(weights, low)


def whole_sum(v):
    return jnp.sum(jnp.sum(v, axis=0, keepdims=True), axis=1, keepdims=True)


def kernel(
    n,
    perm_hbm,
    storage_hbm,
    right_hbm,
    coupling_hbm,
    gains_hbm,
    target_hbm,
    column_hbm,
    out_ref,
    perm_ref,
    storage_ref,
    right_ref,
    gains_ref,
    target_ref,
    column_ref,
    mat,
    coef,
    alpha_ref,
    gamma_ref,
    pivot_ref,
    perm_halo,
    halo_send,
    halo_recv,
    hot_send,
    hot_recv,
    rows_send,
    rows_recv,
    data_send,
    data_recv,
    meta_send,
    meta_recv,
    take_ref,
    give_ref,
    gather_ref,
    scatter_ref,
    gm_ref,
    mat_t,
    load_sem,
    halo_sem,
    hot_sem,
    rows_sem,
    data_sem,
    meta_sem,
):
    me = lax.axis_index("cells")
    chip = me // 2
    core = me % 2
    chips = n // 2
    along_z = chips // ALONG_Y
    z_here = chip // ALONG_Y
    y_here = chip % ALONG_Y
    sibling = chip * 2 + (1 - core)
    left = lax.rem(me + n - 1, n)
    right = lax.rem(me + 1, n)
    height = coef.shape[1]
    half = height // 2
    comp = target_ref.shape[1]
    slots = chips * 8
    steps = alpha_ref.shape[0]

    def greet(device):
        pl.semaphore_signal(
            pltpu.get_barrier_semaphore(),
            inc=1,
            device_id={"cells": device},
            device_id_type=pl.DeviceIdType.MESH,
        )

    def send(src, dst, sems, device):
        copy = pltpu.make_async_remote_copy(
            src_ref=src,
            dst_ref=dst,
            send_sem=sems.at[0],
            recv_sem=sems.at[1],
            device_id={"cells": device},
            device_id_type=pl.DeviceIdType.MESH,
        )
        copy.start()
        return copy

    def await_bytes(ref, sem):
        pltpu.make_async_copy(ref, ref, sem).wait()

    def to_chips(act):
        def plane(j, carry):
            away = along_z // 2 + (j % 2) * (j // 2) - (1 - j % 2) * (j // 2)
            z = lax.rem(z_here + away, along_z)
            for across in (2, 1, 3, 0):
                act(z * ALONG_Y + lax.rem(y_here + across, ALONG_Y))
            return carry

        lax.fori_loop(1, along_z, plane, 0)
        for across in (2, 1, 3):
            act(z_here * ALONG_Y + lax.rem(y_here + across, ALONG_Y))

    to_chips(lambda q: greet(q * 2 + core))
    greet(left)
    greet(right)
    greet(sibling)

    loads = [
        pltpu.make_async_copy(src, dst, load_sem.at[i])
        for i, (src, dst) in enumerate(
            [
                (target_hbm, target_ref),
                (column_hbm, column_ref),
                (perm_hbm, perm_ref),
                (right_hbm, right_ref),
                (storage_hbm, storage_ref),
                (gains_hbm, gains_ref),
                (coupling_hbm, mat),
            ]
        )
    ]
    for load in loads:
        load.start()

    for load in loads[:6]:
        load.wait()
    lane = iota((height, LANES), 1)
    row = iota((height, LANES), 0)
    first_layer = lane < 64
    perm = perm_ref[...].T
    r0 = right_ref[...].T

    t_all = jnp.broadcast_to(target_ref[...].astype(F32), (LANES, LANES))
    c_all = jnp.broadcast_to(column_ref[...].astype(F32), (LANES, LANES))
    t_side = t_all.T
    c_side = c_all.T
    sq_row = iota((LANES, LANES), 0)
    sq_lane = iota((LANES, LANES), 1)
    same = t_all == t_side
    rank_all = jnp.sum(jnp.where(same & (sq_row < sq_lane), 1.0, 0.0), axis=0, keepdims=True)
    rank_side = jnp.sum(jnp.where(same & (sq_lane < sq_row), 1.0, 0.0), axis=1, keepdims=True)

    def parts(target, rank):
        t = target.astype(jnp.int32)
        return lax.shift_right_logical(t, 1), t & 1, rank.astype(jnp.int32)

    q_all, core_all, rank_all = parts(t_all[0:1], rank_all)
    q_side, core_side, rank_side = parts(t_side[:, 0:1], rank_side)
    out_row = q_all * 8 + core_all * 4 + rank_all * 2
    give_ref[...] = jnp.where(
        iota((slots, 2 * comp), 0) == jnp.concatenate([out_row, out_row + 1], axis=1), 1.0, 0.0
    ).astype(BF16)
    in_row = jnp.where(core_side == core, 0, slots) + q_side * 8 + core * 4 + rank_side * 2
    take_ref[...] = jnp.where(
        iota((2 * comp, 2 * slots), 1) == jnp.concatenate([in_row, in_row + 1], axis=0), 1.0, 0.0
    ).astype(BF16)
    weight = jnp.where(core_all == 1, 4.0, 1.0) * jnp.where(rank_all == 1, 2.0, 1.0)
    hot = jnp.where(c_side.astype(jnp.int32) == sq_lane, 1.0, 0.0).astype(BF16)
    codes = nn(jnp.where(iota((chips, comp), 0) == q_all, weight, 0.0).astype(BF16), hot)
    for q in range(chips):
        hot_send[q] = codes[q : q + 1]

    loads[6].wait()
    for g in range(comp // GROUP):
        rows = pl.ds(g * GROUP * 64, GROUP * 64)
        mat_t[:, rows] = mat[rows, :].T

    pl.semaphore_wait(pltpu.get_barrier_semaphore(), chips + 2)

    hot_recv[0, pl.ds(chip, 1)] = hot_send[pl.ds(chip, 1)]
    to_chips(lambda q: send(hot_send.at[q], hot_recv.at[0, chip], hot_sem.at[0], q * 2 + core))
    perm_right = send(
        perm_ref.at[pl.ds(64, 64)], perm_halo.at[pl.ds(0, 64)], halo_sem.at[0], right
    )
    perm_left = send(
        perm_ref.at[pl.ds(0, 64)], perm_halo.at[pl.ds(64, 64)], halo_sem.at[1], left
    )

    trans_in = harmonic(perm, up(perm, 64, 1))
    y_low = jnp.where((lane & 63) == 0, 0.0, harmonic(perm, up(perm, 1, 1)))
    y_high = down(y_low, 1, 1)
    z_low = jnp.where(row == 0, 0.0, harmonic(perm, up(perm, 1)))
    z_high = down(z_low, 1)
    coef[1] = trans_in
    coef[3] = y_low
    coef[4] = y_high
    coef[5] = z_low
    coef[6] = z_high
    part_diag = storage_ref[...].T + trans_in + y_low + y_high + z_low + z_high

    perm_right.wait_recv()
    perm_left.wait_recv()
    trans_out = harmonic(perm, perm_halo[...].T)
    outside = (first_layer & (me == 0)) | (jnp.logical_not(first_layer) & (me == n - 1))
    trans_out = jnp.where(outside, 0.0, trans_out)
    coef[2] = trans_out
    coef[0] = part_diag + trans_out

    a = -z_low
    b = coef[0]
    for s in range(steps):
        k = 1 << s
        rb = 1.0 / b
        scaled = -a * rb
        alpha = -a * up(rb, k)
        gamma = down(scaled, k)
        alpha_ref[s] = alpha
        gamma_ref[s] = gamma
        b = b + down(a * scaled, k) + alpha * a
        if s + 1 < steps:
            a = alpha * up(a, k)
    pivot_ref[...] = 1.0 / b

    def precondition(d):
        for s in range(steps):
            k = 1 << s
            d = d + alpha_ref[s] * up(d, k) + gamma_ref[s] * down(d, k)
        return d * pivot_ref[...]

    def start_halo(v, which):
        top, bottom = v[:half], v[half:]
        low = iota(top.shape, 1) < 64
        halo_send[which, 0] = jnp.where(low, up(top, 64, 1), bottom)
        halo_send[which, 1] = jnp.where(low, top, up(bottom, 64, 1))
        return (
            send(
                halo_send.at[which, 0],
                halo_recv.at[which, 0],
                halo_sem.at[2 + 2 * which],
                right,
            ),
            send(
                halo_send.at[which, 1],
                halo_recv.at[which, 1],
                halo_sem.at[3 + 2 * which],
                left,
            ),
        )

    def stencil(v, which, copies):
        part = (
            coef[0] * v
            - coef[1] * up(v, 64, 1)
            - coef[3] * up(v, 1, 1)
            - coef[4] * down(v, 1, 1)
            - coef[5] * up(v, 1)
            - coef[6] * down(v, 1)
        )
        for copy in copies:
            copy.wait_recv()
        before, after = halo_recv[which, 0], halo_recv[which, 1]
        low = iota(before.shape, 1) < 64
        halo = jnp.concatenate(
            [
                jnp.where(low, before, up(after, 64, 1)),
                jnp.where(low, up(before, 64, 1), after),
            ],
            axis=0,
        )
        return part - coef[2] * halo

    def wells(rows):
        chosen = rows.astype(BF16)
        backs, dot = [], jnp.zeros((8, LANES), F32)
        for g in range(comp // GROUP):
            block = mat[pl.ds(g * GROUP * 64, GROUP * 64), :]
            y = nn(chosen[g * GROUP : (g + 1) * GROUP], mat_t[:, pl.ds(g * GROUP * 64, GROUP * 64)])
            u = (y * gm_ref[pl.ds(g * GROUP, GROUP), :]).astype(BF16)
            backs.append(nn(u, block))
            both = fold(y * u.astype(F32))
            for i in range(0, GROUP * 64, LANES):
                dot = dot + both[:, i : i + LANES]
        return jnp.concatenate(backs, axis=0), dot

    def start_rows(which, v):
        rows_send[which] = v.astype(BF16).reshape(chips, 8, LANES)
        rows_recv[which, 0, pl.ds(chip, 1)] = rows_send[which, pl.ds(chip, 1)]
        to_chips(
            lambda q: send(
                rows_send.at[which, q],
                rows_recv.at[which, 0, chip],
                rows_sem.at[which, 0],
                q * 2 + core,
            )
        )

    def finish_rows(which):
        copy = swap(rows_recv.at[which], rows_sem.at[which])
        total = nn(take_ref[:, :slots], rows_recv[which, 0].reshape(slots, LANES))
        copy.wait_recv()
        return total + nn(take_ref[:, slots:], rows_recv[which, 1].reshape(slots, LANES))

    def start_exchange(which, v, sums):
        largest = jnp.maximum(jnp.max(jnp.max(jnp.abs(v), axis=0, keepdims=True), axis=1, keepdims=True), 1e-30)
        fixed = jnp.round(v * (LARGEST / largest))
        data_send[which] = fixed.astype(jnp.int32).astype(jnp.int16).reshape(chips, 8, LANES)
        at = iota((1, LANES), 1)
        meta = jnp.where(at == 0, largest * (1.0 / LARGEST), 0.0)
        for i, term in enumerate(sums):
            meta = jnp.where(at == i + 1, whole_sum(term), meta)
        meta_send[which] = meta
        data_recv[which, 0, pl.ds(chip, 1)] = data_send[which, pl.ds(chip, 1)]
        meta_recv[which, 0, pl.ds(chip, 1)] = meta[None]

        def act(q):
            send(data_send.at[which, q], data_recv.at[which, 0, chip], data_sem.at[which, 0], q * 2 + core)
            send(meta_send.at[which], meta_recv.at[which, 0, chip], meta_sem.at[which, 0], q * 2 + core)

        to_chips(act)

    def swap(ref, sems):
        await_bytes(ref.at[0, pl.ds(0, chips - 1)], sems.at[0, 1])
        return send(ref.at[0], ref.at[1], sems.at[1], sibling)

    def finish_exchange(which):
        weights = scatter_ref
        data = data_recv.at[which]
        meta = meta_recv.at[which]
        data_swap = swap(data, data_sem.at[which])
        meta_swap = swap(meta, meta_sem.at[which])

        def received(side):
            unit = meta[side][:, :, 0:1]
            v = data[side].astype(jnp.int32).astype(F32) * unit
            return picked(weights[:, side * slots : (side + 1) * slots], v.reshape(slots, LANES))

        total = received(0)
        data_swap.wait_recv()
        meta_swap.wait_recv()
        total = total + received(1)
        sums = jnp.sum(meta[0], axis=0) + jnp.sum(meta[1], axis=0)
        return total, sums

    def drain(ref_one, ref_all, sems):
        await_bytes(ref_all.at[0, pl.ds(0, chips - 1)], sems.at[0, 0])
        await_bytes(ref_one.at[0], sems.at[1, 0])

    def columns_of(v):
        return jnp.concatenate([v[:half].T, v[half:].T], axis=0)

    def side_by_side(v):
        return jnp.concatenate([v[:comp], v[comp:]], axis=1)

    def stacked(v):
        return jnp.concatenate([v[:, :half], v[:, half:]], axis=0)

    z0 = precondition(r0)

    hot_swap = swap(hot_recv, hot_sem)
    z0_cols = columns_of(z0).astype(BF16)
    hot_swap.wait_recv()
    codes = jnp.concatenate([hot_recv[0, :, 0, :], hot_recv[1, :, 0, :]], axis=0).astype(BF16)
    r = iota((slots, 2 * chips), 0)
    source = lax.shift_right_logical(r, 3) + jnp.where(
        (lax.shift_right_logical(r, 2) & 1) == core, 0, chips
    )
    spread = jnp.where(iota((slots, 2 * chips), 1) == source, 1.0, 0.0).astype(BF16)
    r = iota((slots, LANES), 0)
    bit = lax.shift_right_logical(r, 1) & 1
    asked = nn(spread, codes).astype(jnp.int32)
    asked = (lax.shift_right_logical(asked, 2 * core + bit) & 1).astype(F32)
    upper = (r & 1) == 1
    gather_ref[...] = jnp.concatenate(
        [jnp.where(upper, 0.0, asked), jnp.where(upper, asked, 0.0)], axis=1
    ).astype(BF16)
    start_rows(0, nn(gather_ref[...], z0_cols))
    halo0 = start_halo(z0, 0)

    r = iota((2 * chips, 2 * slots), 1)
    spread = jnp.where(
        lax.shift_right_logical(r, 3) == iota((2 * chips, 2 * slots), 0), 1.0, 0.0
    ).astype(BF16)
    asked = nn(codes.astype(F32).T.astype(BF16), spread).astype(jnp.int32)
    r = iota((LANES, 2 * slots), 1)
    bit = lax.shift_right_logical(r, 1) & 1
    mine = (lax.shift_right_logical(r, 2) & 1) == core
    asked = (lax.shift_right_logical(asked, 2 * core + bit) & 1).astype(F32)
    asked = jnp.where(mine, asked, 0.0)
    upper = (r & 1) == 1
    scatter_ref[...] = jnp.concatenate(
        [jnp.where(upper, 0.0, asked), jnp.where(upper, asked, 0.0)], axis=0
    ).astype(BF16)

    gains = gains_ref[...].astype(F32).T.astype(BF16)
    wide = GROUP * 64
    spread = jnp.where((iota((64, wide), 1) & 63) == iota((64, wide), 0), 1.0, 0.0)
    gm_ref[...] = jnp.where(
        (iota((comp, wide), 0) & (GROUP - 1)) == lax.shift_right_logical(iota((comp, wide), 1), 6),
        nn(gains, spread.astype(BF16)),
        0.0,
    )
    s0 = stencil(z0, 0, halo0)
    rz_part = fold(r0 * z0)
    zs_part = fold(z0 * s0)
    back, yu = wells(side_by_side(finish_rows(0)))
    start_exchange(0, picked(give_ref[...], stacked(back)), [rz_part, zs_part + yu])
    added, sums = finish_exchange(0)
    rz0, g00 = sums[:, 1:2], sums[:, 2:3]
    alpha0 = rz0 / g00
    w0 = jnp.concatenate([added[:LANES].T, added[LANES:].T], axis=0)
    q0 = s0 + w0
    r1 = r0 - alpha0 * q0
    z1 = precondition(r1)

    start_rows(1, nn(gather_ref[...], columns_of(z1).astype(BF16)))
    halo1 = start_halo(z1, 1)
    s1 = stencil(z1, 1, halo1)
    fresh_part = fold(r1 * z1)
    zq_part = fold(z1 * q0)
    zs_part = fold(z1 * s1)
    back, yu = wells(side_by_side(finish_rows(1)))
    start_exchange(1, picked(give_ref[...], stacked(back)), [fresh_part, zs_part + yu, zq_part])
    added, sums = finish_exchange(1)
    fresh = sums[:, 1:2]
    beta = fresh / rz0
    alpha1 = fresh / (sums[:, 2:3] + 2.0 * beta * sums[:, 3:4] + beta * beta * g00)
    out_ref[0] = (alpha0 * z0 + alpha1 * (z1 + beta * z0)).T
    w1 = jnp.concatenate([added[:LANES].T, added[LANES:].T], axis=0)
    out_ref[1] = (r1 - alpha1 * (s1 + beta * q0 + w1)).T

    for copy in (perm_right, perm_left, *halo0, *halo1):
        copy.wait_send()
    drain(hot_recv, hot_recv, hot_sem)
    for i in range(2):
        drain(rows_recv.at[i], rows_recv.at[i], rows_sem.at[i])
        drain(data_recv.at[i], data_recv.at[i], data_sem.at[i])
        drain(meta_recv.at[i], meta_recv.at[i], meta_sem.at[i])


def on_device(perm, storage, right_side, coupling, gains, well_target, well_column):
    n = lax.axis_size("cells")
    chips = n // 2
    comp, perforations, height = coupling.shape
    slots = chips * 8
    shape = perm.shape
    columns = shape[0] * shape[1]
    steps = (height - 1).bit_length()

    def flat(x):
        return x.reshape(columns, height)

    vmem = pl.BlockSpec(memory_space=pltpu.VMEM)
    dma = pltpu.SemaphoreType.DMA
    out = pl.pallas_call(
        functools.partial(kernel, n),
        out_shape=jax.ShapeDtypeStruct((2, columns, height), F32),
        in_specs=[pl.BlockSpec(memory_space=pl.ANY)] * 7,
        out_specs=vmem,
        scratch_shapes=[
            pltpu.VMEM((columns, height), F32),
            pltpu.VMEM((columns, height), F32),
            pltpu.VMEM((columns, height), F32),
            pltpu.VMEM((perforations, comp), BF16),
            pltpu.VMEM((1, comp), jnp.int32),
            pltpu.VMEM((1, comp), jnp.int32),
            pltpu.VMEM((comp * perforations, height), BF16),
            pltpu.VMEM((7, height, LANES), F32),
            pltpu.VMEM((steps, height, LANES), F32),
            pltpu.VMEM((steps, height, LANES), F32),
            pltpu.VMEM((height, LANES), F32),
            pltpu.VMEM((columns, height), F32),
            pltpu.VMEM((2, 2, height // 2, LANES), F32),
            pltpu.VMEM((2, 2, height // 2, LANES), F32),
            pltpu.VMEM((chips, 1, LANES), F32),
            pltpu.VMEM((2, chips, 1, LANES), F32),
            pltpu.VMEM((2, chips, 8, LANES), BF16),
            pltpu.VMEM((2, 2, chips, 8, LANES), BF16),
            pltpu.VMEM((2, chips, 8, LANES), jnp.int16),
            pltpu.VMEM((2, 2, chips, 8, LANES), jnp.int16),
            pltpu.VMEM((2, 1, LANES), F32),
            pltpu.VMEM((2, 2, chips, 1, LANES), F32),
            pltpu.VMEM((2 * comp, 2 * slots), BF16),
            pltpu.VMEM((slots, 2 * comp), BF16),
            pltpu.VMEM((slots, 2 * LANES), BF16),
            pltpu.VMEM((2 * LANES, 2 * slots), BF16),
            pltpu.VMEM((comp, GROUP * perforations), F32),
            pltpu.VMEM((height, comp * perforations), BF16),
            dma((7,)),
            dma((6, 2)),
            dma((2, 2)),
            dma((2, 2, 2)),
            dma((2, 2, 2)),
            dma((2, 2, 2)),
        ],
        compiler_params=pltpu.CompilerParams(
            collective_id=0, has_side_effects=True, vmem_limit_bytes=60 * 1024 * 1024
        ),
    )(
        flat(perm),
        flat(storage),
        flat(right_side),
        coupling.reshape(comp * perforations, height),
        gains.T,
        well_target.reshape(1, comp),
        well_column.reshape(1, comp),
    )
    return out[0].reshape(shape), out[1].reshape(shape)


def solution(mesh):
    cells = P(("shift", "cells"), None, None)
    in_specs = (
        cells,
        cells,
        cells,
        P("cells", None, None),
        P("cells", None),
        P("cells", None),
        P("cells"),
    )
    return jax.shard_map(
        on_device, mesh=mesh, in_specs=in_specs, out_specs=(cells, cells), check_vma=False
    )
```
